32 devices in a mesh: groups: 2 (over y), ctx: 8 (over z, x), tp: 2 (over core).
Axes of the slice: x: 2, y: 2, z: 4, core: 2. Of those that a mesh axis runs over, the one named last changes fastest.
Arguments:
- hidden: bfloat16 [4096, 8192], P(('groups', 'ctx'), 'tp'), parts along dimension 0, may hold values from -6 to 6
- queries: bfloat16 [4096, 4096], P(('groups', 'ctx'), 'tp'), parts along dimension 0, may hold values from -300 to 300
- weight_buckets: bfloat16 [16, 512, 4, 2, 128], P('ctx', None, 'tp'), may hold values from -0.0625 to 0.0625
- bucket_rows: int32 [16], replicated, may hold values from 0 to 15, each once
- selected: int32 [8, 3], P('groups'), parts along dimension 0, may hold values from 0 to 3, as said below
- counts: int32 [8], P('groups'), parts along dimension 0, may hold values from 1 to 3, as said below
Outputs:
- attended: bfloat16 [4096, 4096], P(('groups', 'ctx'), 'tp'), parts along dimension 0
The draws below stay inside these ranges and needn't reach their ends.
There are 2 independent parts, one for each index of `groups`. The reference program is written for one: setup_inputs(seed, part) draws one part's arguments, and reference() takes and returns one part's arrays. A program takes and returns all parts, laid end to end along the dimension named above; an argument that names none is the same for every part. Nothing has to cross between parts.
Inputs may be any that keep to these rules, and one draw needn't show every extreme that they name: `selected`: row q begins with q; its next counts[q] - 1 entries are distinct blocks before q; entries past counts[q] are block numbers that are not used. counts[q] is at most min(q + 1, 3); the last query block uses all 3. `bucket_rows`: each row block is stored in exactly one bucket.
All inputs are finite; a program needn't handle non-finite values.
Results may differ from the reference program's by a relative error of at most 0.0028.
The reference program's roundings to bfloat16 on the way count: a program that leaves them out, or rounds other values in their place, can miss the bound.
Values may be sent and summed in bfloat16 or wider, within the bound.
A program may use at most 128 MiB of HBM per device.

```python
import math
import jax
import jax.numpy as jnp
from jax import lax

D = 8192
HD = 128
QH = 32
KVH = 4
KB = 512
TOPK = 3
TOK_DEV = 256
SEQ = 2048
QBLOCKS = 4
BUCKETS = 16
BROWS = 512
N_CTX = 8


def draw_queries(key, part):
    key = jax.random.fold_in(key, 11)
    first_key = jax.random.fold_in(key, 0)
    base = jax.random.normal(first_key, (SEQ, QH * HD), jnp.float32)
    values = jnp.clip(base * 2.0, -10.0, 10.0)
    return values.astype(jnp.bfloat16)


def draw_selected(key, part):
    key = jax.random.fold_in(key, 22)
    raw = jax.random.randint(key, (QBLOCKS, QBLOCKS), 0, 1 << 20)
    columns = jnp.arange(QBLOCKS, dtype=jnp.int32)[None, :]
    owners = jnp.arange(QBLOCKS, dtype=jnp.int32)[:, None]
    ranked = raw * QBLOCKS + columns
    ranked = jnp.where(columns < owners, ranked, -1 - columns)
    chosen = lax.top_k(ranked, TOPK - 1)[1].astype(jnp.int32)
    return jnp.concatenate([owners, chosen], axis=1).astype(jnp.int32)


def draw_counts(key, part):
    key = jax.random.fold_in(key, 33)
    ceiling = jnp.minimum(jnp.arange(QBLOCKS, dtype=jnp.int32) + 1, TOPK)
    drawn = jax.random.randint(key, (QBLOCKS,), 1, ceiling + 1)
    return drawn.at[QBLOCKS - 1].set(TOPK).astype(jnp.int32)


def levels(rng, extent, shards, low, high):
    loudness = 1.0
    for axis_at, shards_of in shards:
        heights = jax.random.uniform(jax.random.fold_in(jax.random.fold_in(rng, 6), axis_at), (shards_of,), jnp.float32, low / len(shards), high / len(shards))
        loudness = loudness * jnp.repeat(jnp.exp(heights), extent[axis_at] // shards_of).reshape((-1,) + (1,) * (len(extent) - 1 - axis_at))
    return loudness


def scatter_about(stream_key, shape, width, limit, cuts=(), kind=jnp.bfloat16):
    array = width * jax.random.normal(stream_key, shape, jnp.float32)
    if cuts:
        array = array * levels(stream_key, shape, cuts, -0.22, 0.18)
    return jnp.clip(array, -limit, limit).astype(kind)


def setup_inputs(seed: int = 0, part: int = 0) -> dict:
    key_of = jax.random.split(jax.random.key(seed), 7)
    part_keys = jax.random.split(jax.random.fold_in(key_of[6], part), 7)
    return {
        "hidden": scatter_about(part_keys[0], (SEQ, D), 1.0, 6.0, ((0, 8), (1, 2))),
        "queries": draw_queries(jax.random.fold_in(jax.random.fold_in(key_of[6], part), 71), part),
        "weight_buckets": scatter_about(key_of[2], (BUCKETS, BROWS, KVH, 2, HD), D ** -0.5, 0.0625, ((0, 8), (2, 2))),
        "bucket_rows": jax.random.permutation(key_of[3], BUCKETS).astype(jnp.int32),
        "selected": draw_selected(jax.random.fold_in(jax.random.fold_in(key_of[6], part), 71), part),
        "counts": draw_counts(jax.random.fold_in(jax.random.fold_in(key_of[6], part), 71), part),
    }


masked_score = -1e+30

def reference(hidden, queries, weight_buckets, bucket_rows, selected, counts):
    seq_len = TOK_DEV * N_CTX
    kv_width = KVH * 2 * HD
    ordered = hidden.reshape(N_CTX, TOK_DEV, D).transpose(1, 0, 2).reshape(seq_len, D)
    placed = jnp.zeros((BUCKETS, BROWS, kv_width), jnp.bfloat16)
    placed = placed.at[bucket_rows].set(weight_buckets.reshape(BUCKETS, BROWS, kv_width))
    key_values = jnp.dot(ordered, placed.reshape(D, kv_width), preferred_element_type=jnp.float32)
    key_values = key_values.astype(jnp.bfloat16).reshape(QBLOCKS, KB, KVH, 2, HD)
    group_size = QH // KVH
    score_scale = 1.0 / math.sqrt(HD)
    offsets = jnp.arange(KB, dtype=jnp.int32)

    def one_block(query_block):
        rows_here = lax.dynamic_slice_in_dim(queries, query_block * KB, KB, 0)
        rows_here = rows_here.reshape(KB, KVH, group_size, HD).astype(jnp.float32)
        query_pos = query_block * KB + offsets
        peaks = []
        totals = []
        blends = []
        for column in range(TOPK):
            key_block = selected[query_block, column]
            is_live = column < counts[query_block]
            stacked = key_values[key_block].astype(jnp.float32)
            key_pos = key_block * KB + offsets
            scores = jnp.einsum('qkgd,skd->kgqs', rows_here, stacked[:, :, 0]) * score_scale
            visible = (key_pos[None, :] <= query_pos[:, None]) & is_live
            scores = jnp.where(visible, scores, masked_score)
            peak = scores.max(axis=-1)
            raised = jnp.exp(scores - peak[..., None])
            total = raised.sum(axis=-1)
            weights = lax.optimization_barrier(raised.astype(jnp.bfloat16)).astype(jnp.float32)
            blended = jnp.einsum('kgqs,skd->kgqd', weights, stacked[:, :, 1])
            peaks.append(peak)
            totals.append(total)
            blends.append(blended)
        peaks = jnp.stack(peaks)
        totals = jnp.stack(totals)
        blends = jnp.stack(blends)
        highest = peaks.max(axis=0, keepdims=True)
        factors = jnp.exp(peaks - highest)
        weighted = lax.optimization_barrier(jnp.sum(factors[..., None] * blends, axis=0))
        normalizer = lax.optimization_barrier(jnp.sum(factors * totals, axis=0))
        result = weighted / normalizer[..., None]
        return result.transpose(2, 0, 1, 3).reshape(KB, QH * HD).astype(jnp.bfloat16)
    outputs = lax.map(one_block, jnp.arange(QBLOCKS, dtype=jnp.int32))
    return outputs.reshape(seq_len, QH * HD)
```

```python
import functools
import math

import jax
import jax.numpy as jnp
from jax import lax
from jax.experimental import pallas as pl
from jax.experimental.pallas import tpu as pltpu
from jax.sharding import PartitionSpec as P

HD = 128
KB = 512
TOPK = 3


masked_score = -1e30


def general_shards(hidden, queries, weight_buckets, bucket_rows, selected, counts):
    tok_rows = hidden.shape[0]
    ctx_size = lax.axis_size("ctx")
    ctx_index = lax.axis_index("ctx")
    gathered = lax.all_gather(hidden, "tp", axis=1, tiled=True)
    feat_width = gathered.shape[1]
    bucket_count = bucket_rows.shape[0]
    bucket_depth = feat_width // bucket_count
    kv_local = weight_buckets.shape[2]
    kv_width = kv_local * 2 * HD
    arranged = gathered.reshape(tok_rows, bucket_count, bucket_depth)[:, bucket_rows, :]
    arranged = arranged.reshape(tok_rows, feat_width)
    piece = lax.all_gather(weight_buckets, "ctx", axis=0, tiled=True)
    count_rows = piece.shape[0] * bucket_depth
    projected = jnp.dot(
        arranged, piece.reshape(count_rows, kv_width), preferred_element_type=jnp.float32
    )
    key_values = projected.astype(jnp.bfloat16)
    block_count = selected.shape[0]
    block_rows = tok_rows // block_count
    by_block = key_values.reshape(block_count, block_rows, kv_width)
    query_blocks = max(1, tok_rows // KB)
    query_len = min(KB, tok_rows)
    targets = (jnp.arange(ctx_size, dtype=jnp.int32) * tok_rows // KB)[:, None] + jnp.arange(
        query_blocks, dtype=jnp.int32
    )[None, :]
    wanted = selected[targets].reshape(ctx_size, query_blocks * TOPK)
    live = jnp.arange(TOPK, dtype=jnp.int32)[None, None, :] < counts[targets][:, :, None]
    block_tags = jnp.where(live.reshape(ctx_size, query_blocks * TOPK), wanted, -1)
    local_tags = jnp.broadcast_to(
        jnp.arange(query_blocks, dtype=jnp.int32)[:, None], (query_blocks, TOPK)
    )
    local_tags = jnp.broadcast_to(local_tags, block_tags.shape)
    markers = jnp.stack([block_tags, local_tags], axis=-1).astype(jnp.bfloat16)
    outgoing = by_block[wanted]
    heads_local = queries.shape[1] // HD
    group_size = heads_local // kv_local
    score_scale = 1.0 / math.sqrt(HD)
    offsets = jnp.arange(KB, dtype=jnp.int32)
    within = offsets % block_rows * ctx_size + offsets // block_rows
    query_offsets = jnp.arange(query_len, dtype=jnp.int32)

    def one_item(payload, marker):
        block_id = marker[0].astype(jnp.int32)
        is_live = block_id >= 0
        key_block = jnp.maximum(block_id, 0)
        which_block = marker[1].astype(jnp.int32)
        stacked = payload.reshape(KB, kv_local, 2, HD)
        key_pos = key_block * KB + within
        rows_here = queries
        rows_here = rows_here.reshape(query_len, kv_local, group_size, HD)
        query_pos = ctx_index * tok_rows + which_block * query_len + query_offsets
        scores = (
            jnp.einsum(
                "qkgd,skd->kgqs", rows_here, stacked[:, :, 0], preferred_element_type=jnp.float32
            )
            * score_scale
        )
        visible = (key_pos[None, :] <= query_pos[:, None]) & is_live
        scores = jnp.where(visible, scores, masked_score)
        peak = scores.max(axis=-1)
        raised = jnp.exp(scores - peak[..., None])
        total = raised.sum(axis=-1)
        blended = jnp.einsum(
            "kgqs,skd->kgqd",
            raised.astype(jnp.bfloat16),
            stacked[:, :, 1],
            preferred_element_type=jnp.float32,
        )
        return (peak, total, blended)

    payloads = lax.all_to_all(outgoing, "ctx", split_axis=0, concat_axis=0, tiled=True)
    markings = lax.all_to_all(markers, "ctx", split_axis=0, concat_axis=0, tiled=True)

    def handle(position):
        payload = lax.dynamic_index_in_dim(payloads, position, 1, keepdims=False)
        marker = lax.dynamic_index_in_dim(markings[0], position, 0, keepdims=False)
        return one_item(payload, marker)

    peaks, totals, blends = lax.map(handle, jnp.arange(payloads.shape[1], dtype=jnp.int32))
    peaks = peaks.reshape(query_blocks, TOPK, kv_local, group_size, query_len)
    totals = totals.reshape(query_blocks, TOPK, kv_local, group_size, query_len)
    blends = blends.reshape(query_blocks, TOPK, kv_local, group_size, query_len, HD)
    highest = peaks.max(axis=1, keepdims=True)
    factors = jnp.exp(peaks - highest)
    weighted = jnp.sum(factors[..., None] * blends, axis=1)
    normalizer = jnp.sum(factors * totals, axis=1)
    result = weighted / normalizer[..., None]
    return result.transpose(0, 3, 1, 2, 4).reshape(tok_rows, heads_local * HD).astype(jnp.bfloat16)


SUB = 16
MESH = pl.DeviceIdType.MESH
MIB = 1 << 20


def ring_to_ctx(pos, n):
    upper = pos // (n // 2)
    return 2 * pos + upper * (2 * n - 1 - 4 * pos)


def ctx_to_ring(ctx, n):
    return ctx // 2 + (ctx % 2) * (n - 1 - 2 * (ctx // 2))


def job_table(rows):
    units = rows // SUB
    first = (units + 5) // 6
    second = (units - 4 * first) // 2
    sizes = [first, second, first, first, second, first]
    starts = [sum(sizes[:i]) for i in range(6)]
    jobs = []
    for i in range(4):
        jobs.append((sizes[i] * SUB, starts[i] * SUB, starts[5 - i] * SUB))
    return jobs


def project_kernel(
    n, kv_rows_piece, rows_ref, hidden_ref, w_ref, kv_ref,
    feats, wbuf, acc, hid_sem, w_send, w_recv, y_send, y_recv, kv_send, kv_recv,
):
    ctx = lax.axis_index("ctx")
    group = lax.axis_index("groups")
    core = lax.axis_index("tp")
    pos = ctx_to_ring(ctx, n)
    nxt = ring_to_ctx((pos + 1) % n, n)
    prv = ring_to_ctx((pos + n - 1) % n, n)
    other_core = {"tp": 1 - core}
    other_group = {"groups": 1 - group}
    depth = feats.shape[2]
    in_half = feats.shape[0] // 2
    per_owner = rows_ref.shape[0] // n

    barrier = pltpu.get_barrier_semaphore()
    for peer in ({"ctx": nxt}, {"ctx": prv}, other_core, other_group):
        pl.semaphore_signal(barrier, inc=1, device_id=peer, device_id_type=MESH)
    pl.semaphore_wait(barrier, 4)

    jobs = job_table(w_ref.shape[0])
    forward = (True, False, False, True)

    def ring_copy(k, step):
        size, low, high = jobs[k]
        rows = pl.ds(pl.multiple_of(low + group * (high - low), SUB), size)
        if forward[k]:
            origin, peer = (pos + n - step) % n, nxt
        else:
            origin, peer = (pos + step) % n, prv
        source = w_ref.at[rows] if step == 0 else wbuf.at[origin, rows]
        return pltpu.make_async_remote_copy(
            src_ref=source, dst_ref=wbuf.at[origin, rows],
            send_sem=w_send.at[k, step], recv_sem=w_recv.at[k, step],
            device_id={"ctx": peer}, device_id_type=MESH,
        )

    def plane_copy(k, step):
        size, low, high = jobs[k]
        rows = pl.ds(pl.multiple_of(low + group * (high - low), SUB), size)
        origin = (pos + n - 1 - step) % n if forward[k] else (pos + 1 + step) % n
        return pltpu.make_async_remote_copy(
            src_ref=wbuf.at[origin, rows], dst_ref=wbuf.at[origin, rows],
            send_sem=y_send.at[k, step], recv_sem=y_recv.at[k, step],
            device_id=other_group, device_id_type=MESH,
        )

    rings = [[ring_copy(k, s) for s in range(n - 1)] for k in range(4)]
    planes = [[plane_copy(k, s) for s in range(n - 1)] for k in range(2)]
    for k in range(4):
        rings[k][0].start()

    def hidden_copies(i):
        source = hidden_ref.at[:, pl.ds(i * depth, depth)]
        mine = feats.at[core * in_half + i]
        swap = pltpu.make_async_remote_copy(
            src_ref=source, dst_ref=mine, send_sem=hid_sem.at[0, i], recv_sem=hid_sem.at[1, i],
            device_id=other_core, device_id_type=MESH,
        )
        return swap, pltpu.make_async_copy(source, mine, hid_sem.at[2, i])

    for i in range(in_half):
        for copy in hidden_copies(i):
            copy.start()

    def consume(origin, chunk, first=False):
        owner = ring_to_ctx(origin, n)
        for j in range(per_owner):
            row = rows_ref[owner * per_owner + j]
            part = feats[row]
            term = jnp.dot(
                part, chunk[j * depth : (j + 1) * depth, :], preferred_element_type=jnp.float32
            )
            if first and j == 0:
                acc[...] = term
            else:
                acc[...] += term

    done = {}
    for distance in range(1, n):
        done.setdefault(max(distance - 1, n - 1 - distance), []).append(distance)

    for step in range(n - 1):
        for k in range(4):
            rings[k][step].wait_recv()
            if step + 1 < n - 1:
                rings[k][step + 1].start()
            if k < 2:
                planes[k][step].start()
        if step == 0:
            for i in range(in_half):
                for copy in hidden_copies(i):
                    copy.wait()
            consume(pos, w_ref, True)
        if step > 0:
            for k in range(2):
                planes[k][step - 1].wait_recv()
            for distance in done.get(step - 1, ()):
                origin = (pos + n - distance) % n
                consume(origin, wbuf.at[origin])
    for k in range(2):
        planes[k][n - 2].wait_recv()
    for distance in done.get(n - 2, ()):
        origin = (pos + n - distance) % n
        consume(origin, wbuf.at[origin])
    for k in range(4):
        for s in range(n - 1):
            rings[k][s].wait_send()
    for k in range(2):
        for s in range(n - 1):
            planes[k][s].wait_send()

    kv_ref[ctx] = acc[...].astype(kv_ref.dtype)
    pieces = kv_ref.shape[1] // kv_rows_piece

    def kv_copy(k, step):
        rows = pl.ds(k * kv_rows_piece, kv_rows_piece)
        if k % 2 == 0:
            origin, peer = ring_to_ctx((pos + n - step) % n, n), nxt
        else:
            origin, peer = ring_to_ctx((pos + step) % n, n), prv
        return pltpu.make_async_remote_copy(
            src_ref=kv_ref.at[origin, rows], dst_ref=kv_ref.at[origin, rows],
            send_sem=kv_send.at[k, step], recv_sem=kv_recv.at[k, step],
            device_id={"ctx": peer}, device_id_type=MESH,
        )

    moves = [[kv_copy(k, s) for s in range(n - 1)] for k in range(pieces)]
    for k in range(pieces):
        moves[k][0].start()
    for step in range(n - 1):
        for k in range(pieces):
            moves[k][step].wait_recv()
            if step + 1 < n - 1:
                moves[k][step + 1].start()
    for k in range(pieces):
        for s in range(n - 1):
            moves[k][s].wait_send()


def attend_kernel(n, sel_ref, cnt_ref, at_ref, q_ref, kv_ref, out_ref):
    tok_rows = q_ref.shape[0]
    block_rows = KB // n
    start = at_ref[0] * tok_rows
    q_block = start // KB
    q = q_ref[...]
    scale = 1.0 / math.sqrt(HD)
    offsets = lax.broadcasted_iota(jnp.int32, (KB, 1), 0)
    within = offsets % block_rows * n + offsets // block_rows
    q_within = start % KB + lax.broadcasted_iota(jnp.int32, (1, tok_rows), 1)

    def load(block):
        rows = pl.ds(pl.multiple_of(block * block_rows, block_rows), block_rows)
        k = kv_ref[:, rows, :HD].reshape(KB, HD)
        v = kv_ref[:, rows, HD:].reshape(KB, HD)
        return k, v

    def item(block, masked):
        k, v = load(block)
        s = lax.dot_general(k, q, (((1,), (1,)), ((), ())), preferred_element_type=jnp.float32)
        s = s * scale
        if masked:
            s = jnp.where(within <= q_within, s, masked_score)
        peak = jnp.max(s, axis=0, keepdims=True)
        raised = jnp.exp(s - peak)
        total = jnp.sum(raised, axis=0, keepdims=True)
        blended = lax.dot_general(
            v, raised.astype(jnp.bfloat16), (((0,), (0,)), ((), ())),
            preferred_element_type=jnp.float32,
        )
        return peak, total, blended

    def more(c, carry):
        top, total, blended = carry
        peak_c, total_c, blended_c = item(sel_ref[q_block, c], False)
        new = jnp.maximum(top, peak_c)
        old_f = jnp.exp(top - new)
        new_f = jnp.exp(peak_c - new)
        return new, total * old_f + total_c * new_f, blended * old_f + blended_c * new_f

    carry = item(q_block, True)
    top, total, blended = lax.fori_loop(1, cnt_ref[q_block], more, carry)
    out_ref[...] = (blended / total).T.astype(out_ref.dtype)


def ladder_shards(hidden, queries, weight_buckets, bucket_rows, selected, counts):
    n = lax.axis_size("ctx")
    tok_rows, half = hidden.shape
    feat_width = half * lax.axis_size("tp")
    kv_local = weight_buckets.shape[2]
    kv_width = kv_local * 2 * HD
    w = weight_buckets.reshape(-1, kv_width)
    chunk_rows = w.shape[0]
    piece = tok_rows // 4
    vmem = pl.BlockSpec(memory_space=pltpu.VMEM)
    smem = pl.BlockSpec(memory_space=pltpu.SMEM)
    dma = pltpu.SemaphoreType.DMA
    kv = pl.pallas_call(
        functools.partial(project_kernel, n, piece),
        out_shape=jax.ShapeDtypeStruct((n, tok_rows, kv_width), jnp.bfloat16),
        in_specs=[smem, vmem, vmem],
        out_specs=vmem,
        scratch_shapes=[
            pltpu.VMEM((bucket_rows.shape[0], tok_rows, feat_width // bucket_rows.shape[0]), jnp.bfloat16),
            pltpu.VMEM((n, chunk_rows, kv_width), jnp.bfloat16),
            pltpu.VMEM((tok_rows, kv_width), jnp.float32),
            dma((3, bucket_rows.shape[0] // 2)),
            dma((4, n - 1)), dma((4, n - 1)),
            dma((2, n - 1)), dma((2, n - 1)),
            dma((4, n - 1)), dma((4, n - 1)),
        ],
        compiler_params=pltpu.CompilerParams(
            collective_id=0, has_side_effects=True, vmem_limit_bytes=40 * MIB
        ),
        name="project",
    )(bucket_rows, hidden, w)

    heads = queries.shape[1] // HD
    group = heads // kv_local
    here = lax.axis_index("ctx").astype(jnp.int32).reshape(1)
    return pl.pallas_call(
        functools.partial(attend_kernel, n),
        out_shape=jax.ShapeDtypeStruct(queries.shape, jnp.bfloat16),
        grid_spec=pltpu.PrefetchScalarGridSpec(
            num_scalar_prefetch=3,
            grid=(heads,),
            in_specs=[
                pl.BlockSpec((tok_rows, HD), lambda h, *_: (0, h)),
                pl.BlockSpec((n, tok_rows, 2 * HD), lambda h, *_: (0, 0, h // group)),
            ],
            out_specs=pl.BlockSpec((tok_rows, HD), lambda h, *_: (0, h)),
        ),
        compiler_params=pltpu.CompilerParams(vmem_limit_bytes=40 * MIB),
        name="attend",
    )(selected, counts, here, queries, kv)


def takes_ladder(mesh, hidden, weight_buckets, selected):
    shape = mesh.shape
    if shape["groups"] != 2 or shape["tp"] != 2 or shape["ctx"] % 2 or shape["ctx"] > 16:
        return False
    tok_rows = hidden.shape[0] // (shape["groups"] * shape["ctx"])
    block_rows = KB // shape["ctx"]
    return KB % tok_rows == 0 and block_rows % SUB == 0 and tok_rows % (4 * SUB) == 0


def solution(mesh):
    placed = (
        P(("groups", "ctx"), "tp"),
        P(("groups", "ctx"), "tp"),
        P("ctx", None, "tp", None, None),
        P(),
        P("groups", None),
        P("groups"),
    )

    def run(hidden, queries, weight_buckets, bucket_rows, selected, counts):
        body = ladder_shards if takes_ladder(mesh, hidden, weight_buckets, selected) else general_shards
        return jax.shard_map(
            body, mesh=mesh, in_specs=placed, out_specs=P(("groups", "ctx"), "tp"), check_vma=False
        )(hidden, queries, weight_buckets, bucket_rows, selected, counts)

    return run
```

```python
import functools
import math

import jax
import jax.numpy as jnp
from jax import lax
from jax.experimental import pallas as pl
from jax.experimental.pallas import tpu as pltpu
from jax.sharding import PartitionSpec as P

HD = 128
KB = 512
TOPK = 3


masked_score = -1e30


def general_shards(hidden, queries, weight_buckets, bucket_rows, selected, counts):
    tok_rows = hidden.shape[0]
    ctx_size = lax.axis_size("ctx")
    ctx_index = lax.axis_index("ctx")
    gathered = lax.all_gather(hidden, "tp", axis=1, tiled=True)
    feat_width = gathered.shape[1]
    bucket_count = bucket_rows.shape[0]
    bucket_depth = feat_width // bucket_count
    kv_local = weight_buckets.shape[2]
    kv_width = kv_local * 2 * HD
    arranged = gathered.reshape(tok_rows, bucket_count, bucket_depth)[:, bucket_rows, :]
    arranged = arranged.reshape(tok_rows, feat_width)
    piece = lax.all_gather(weight_buckets, "ctx", axis=0, tiled=True)
    count_rows = piece.shape[0] * bucket_depth
    projected = jnp.dot(
        arranged, piece.reshape(count_rows, kv_width), preferred_element_type=jnp.float32
    )
    key_values = projected.astype(jnp.bfloat16)
    block_count = selected.shape[0]
    block_rows = tok_rows // block_count
    by_block = key_values.reshape(block_count, block_rows, kv_width)
    query_blocks = max(1, tok_rows // KB)
    query_len = min(KB, tok_rows)
    targets = (jnp.arange(ctx_size, dtype=jnp.int32) * tok_rows // KB)[:, None] + jnp.arange(
        query_blocks, dtype=jnp.int32
    )[None, :]
    wanted = selected[targets].reshape(ctx_size, query_blocks * TOPK)
    live = jnp.arange(TOPK, dtype=jnp.int32)[None, None, :] < counts[targets][:, :, None]
    block_tags = jnp.where(live.reshape(ctx_size, query_blocks * TOPK), wanted, -1)
    local_tags = jnp.broadcast_to(
        jnp.arange(query_blocks, dtype=jnp.int32)[:, None], (query_blocks, TOPK)
    )
    local_tags = jnp.broadcast_to(local_tags, block_tags.shape)
    markers = jnp.stack([block_tags, local_tags], axis=-1).astype(jnp.bfloat16)
    outgoing = by_block[wanted]
    heads_local = queries.shape[1] // HD
    group_size = heads_local // kv_local
    score_scale = 1.0 / math.sqrt(HD)
    offsets = jnp.arange(KB, dtype=jnp.int32)
    within = offsets % block_rows * ctx_size + offsets // block_rows
    query_offsets = jnp.arange(query_len, dtype=jnp.int32)

    def one_item(payload, marker):
        block_id = marker[0].astype(jnp.int32)
        is_live = block_id >= 0
        key_block = jnp.maximum(block_id, 0)
        which_block = marker[1].astype(jnp.int32)
        stacked = payload.reshape(KB, kv_local, 2, HD)
        key_pos = key_block * KB + within
        rows_here = queries
        rows_here = rows_here.reshape(query_len, kv_local, group_size, HD)
        query_pos = ctx_index * tok_rows + which_block * query_len + query_offsets
        scores = (
            jnp.einsum(
                "qkgd,skd->kgqs", rows_here, stacked[:, :, 0], preferred_element_type=jnp.float32
            )
            * score_scale
        )
        visible = (key_pos[None, :] <= query_pos[:, None]) & is_live
        scores = jnp.where(visible, scores, masked_score)
        peak = scores.max(axis=-1)
        raised = jnp.exp(scores - peak[..., None])
        total = raised.sum(axis=-1)
        blended = jnp.einsum(
            "kgqs,skd->kgqd",
            raised.astype(jnp.bfloat16),
            stacked[:, :, 1],
            preferred_element_type=jnp.float32,
        )
        return (peak, total, blended)

    payloads = lax.all_to_all(outgoing, "ctx", split_axis=0, concat_axis=0, tiled=True)
    markings = lax.all_to_all(markers, "ctx", split_axis=0, concat_axis=0, tiled=True)

    def handle(position):
        payload = lax.dynamic_index_in_dim(payloads, position, 1, keepdims=False)
        marker = lax.dynamic_index_in_dim(markings[0], position, 0, keepdims=False)
        return one_item(payload, marker)

    peaks, totals, blends = lax.map(handle, jnp.arange(payloads.shape[1], dtype=jnp.int32))
    peaks = peaks.reshape(query_blocks, TOPK, kv_local, group_size, query_len)
    totals = totals.reshape(query_blocks, TOPK, kv_local, group_size, query_len)
    blends = blends.reshape(query_blocks, TOPK, kv_local, group_size, query_len, HD)
    highest = peaks.max(axis=1, keepdims=True)
    factors = jnp.exp(peaks - highest)
    weighted = jnp.sum(factors[..., None] * blends, axis=1)
    normalizer = jnp.sum(factors * totals, axis=1)
    result = weighted / normalizer[..., None]
    return result.transpose(0, 3, 1, 2, 4).reshape(tok_rows, heads_local * HD).astype(jnp.bfloat16)


SUB = 16
MESH = pl.DeviceIdType.MESH
MIB = 1 << 20


def ladder_ctx(pos, n):
    upper = pos // (n // 2)
    return 2 * pos + upper * (2 * n - 1 - 4 * pos)


def ladder_pos(ctx, n):
    return ctx // 2 + (ctx % 2) * (n - 1 - 2 * (ctx // 2))


def project_kernel(
    n, rows_ref, hidden_ref, w_ref, kv_ref,
    feats, xfeats, stage, wbuf, acc, psend, precv,
    hid_sem, w_send, w_recv, x_send, x_recv, f_send, f_recv, p_send, p_recv, kv_send, kv_recv, own_sem,
):
    ctx = lax.axis_index("ctx")
    plane = lax.axis_index("groups")
    core = lax.axis_index("tp")
    col = ctx % 2
    pos = plane * (n - 1) + (ctx // 2) * (1 - 2 * plane)
    walk = ladder_pos(ctx, n)
    after = ladder_ctx((walk + 1) % n, n)
    before = ladder_ctx((walk + n - 1) % n, n)
    depth = feats.shape[2]
    width = wbuf.shape[3]
    in_half = feats.shape[0] // 2
    share = n // 2

    def node(p):
        side = p // (n // 2)
        return side, p * (1 - 2 * side) + side * (n - 1)

    def bucket(p, column):
        side, level = node(p)
        return (level * 2 + column) * 2 + side

    def ring_peer(p):
        side, level = node(p)
        return {"ctx": level * 2 + col, "groups": side}

    up, down = ring_peer((pos + 1) % n), ring_peer((pos + n - 1) % n)
    other_core = {"tp": 1 - core}
    other_col = {"ctx": ctx + 1 - 2 * col}

    barrier = pltpu.get_barrier_semaphore()
    peers = (up, down, other_core, other_col, {"ctx": after}, {"ctx": before})
    for peer in peers:
        pl.semaphore_signal(barrier, inc=1, device_id=peer, device_id_type=MESH)
    pl.semaphore_wait(barrier, len(peers))

    piece = depth // 4

    def weight_copy(c, k, step):
        rows = pl.ds(k * piece, piece)
        if k < 2:
            origin, peer = (pos + n - step) % n, up
        else:
            origin, peer = (pos + step) % n, down
        if step == 0:
            source = w_ref.at[plane, rows, pl.ds(c * width, width)]
        else:
            source = wbuf.at[c, origin, rows]
        return pltpu.make_async_remote_copy(
            src_ref=source, dst_ref=wbuf.at[c, origin, rows],
            send_sem=w_send.at[c, k, step], recv_sem=w_recv.at[c, k, step],
            device_id=peer, device_id_type=MESH,
        )

    def weight_start(c):
        for k in range(4):
            weight_copy(c, k, 0).start()

    def weight_step(c, step):
        for k in range(4):
            weight_copy(c, k, step).wait_recv()
            if step + 1 < n - 1:
                weight_copy(c, k, step + 1).start()

    def own_copy(c):
        return pltpu.make_async_copy(
            w_ref.at[plane, :, pl.ds(c * width, width)], wbuf.at[c, pos], own_sem.at[c]
        )

    def hidden_copies(i):
        source = hidden_ref.at[:, pl.ds(i * depth, depth)]
        mine = feats.at[core * in_half + i]
        swap = pltpu.make_async_remote_copy(
            src_ref=source, dst_ref=mine, send_sem=hid_sem.at[0, i], recv_sem=hid_sem.at[1, i],
            device_id=other_core, device_id_type=MESH,
        )
        return swap, pltpu.make_async_copy(source, mine, hid_sem.at[2, i])

    def across_copy(i):
        return pltpu.make_async_remote_copy(
            src_ref=stage.at[i], dst_ref=xfeats.at[core * share + i],
            send_sem=x_send.at[i], recv_sem=x_recv.at[i],
            device_id=other_col, device_id_type=MESH,
        )

    def pass_copy(i):
        spot = xfeats.at[core * share + i]
        return pltpu.make_async_remote_copy(
            src_ref=spot, dst_ref=spot, send_sem=f_send.at[i], recv_sem=f_recv.at[i],
            device_id=other_core, device_id_type=MESH,
        )

    def partial_copy(c):
        return pltpu.make_async_remote_copy(
            src_ref=psend.at[c], dst_ref=precv.at[c], send_sem=p_send.at[c], recv_sem=p_recv.at[c],
            device_id=other_col, device_id_type=MESH,
        )

    block_rows = KB // n

    def kv_copy(c, k, step):
        rows = pl.ds(k * block_rows, block_rows)
        if k % 2 == 0:
            origin, peer = ladder_ctx((walk + n - step) % n, n), after
        else:
            origin, peer = ladder_ctx((walk + step) % n, n), before
        spot = kv_ref.at[c, origin, rows]
        return pltpu.make_async_remote_copy(
            src_ref=spot, dst_ref=spot, send_sem=kv_send.at[c, k, step], recv_sem=kv_recv.at[c, k, step],
            device_id={"ctx": peer}, device_id_type=MESH,
        )

    pieces = kv_ref.shape[2] // block_rows

    def partials(c):
        psend[c] = jnp.zeros(psend.shape[1:], jnp.float32)

        @pl.loop(0, n)
        def _(p):
            psend[c] += jnp.dot(xfeats[p], wbuf[c, p], preferred_element_type=jnp.float32)

        partial_copy(c).start()
        acc[c] = jnp.zeros(acc.shape[1:], jnp.float32)

        @pl.loop(0, n)
        def _(p):
            row = rows_ref[bucket(p, col)]
            acc[c] += jnp.dot(feats[row], wbuf[c, p], preferred_element_type=jnp.float32)

    def kv_start(c):
        partial_copy(c).wait_recv()
        kv_ref[c, ctx] = (acc[c] + precv[c]).astype(kv_ref.dtype)
        for k in range(pieces):
            kv_copy(c, k, 0).start()

    def kv_step(c, step):
        for k in range(pieces):
            kv_copy(c, k, step).wait_recv()
            if step + 1 < n - 1:
                kv_copy(c, k, step + 1).start()

    weight_start(0)
    for i in range(in_half):
        for copy in hidden_copies(i):
            copy.start()
    for c in range(2):
        own_copy(c).start()
    steps = n - 1
    lag = steps - 1
    for t in range(steps + lag):
        if t < steps:
            weight_step(0, t)
        if t + 1 == lag:
            weight_start(1)
        if t >= lag:
            weight_step(1, t - lag)
        if t == 1:
            for i in range(in_half):
                for copy in hidden_copies(i):
                    copy.wait()
            for i in range(share):
                stage[i] = feats[rows_ref[bucket(core * share + i, 1 - col)]]
                across_copy(i).start()
        if t == lag + 3:
            for i in range(share):
                across_copy(i).wait_recv()
                pass_copy(i).start()
            for c in range(2):
                own_copy(c).wait()
        if t == lag + 4:
            for i in range(share):
                pass_copy(i).wait_recv()
            partials(0)
    partials(1)
    kv_start(0)
    kv_lag = 3
    for t in range(steps + kv_lag):
        if t < steps:
            kv_step(0, t)
        if t + 1 == kv_lag:
            kv_start(1)
        if t >= kv_lag:
            kv_step(1, t - kv_lag)

    for i in range(share):
        across_copy(i).wait_send()
        pass_copy(i).wait_send()
    for c in range(2):
        partial_copy(c).wait_send()
        for s in range(steps):
            for k in range(4):
                weight_copy(c, k, s).wait_send()
            for k in range(pieces):
                kv_copy(c, k, s).wait_send()


def attend_kernel(n, sel_ref, cnt_ref, at_ref, q_ref, kv_ref, out_ref):
    tok_rows = q_ref.shape[0]
    block_rows = KB // n
    start = at_ref[0] * tok_rows
    q_block = start // KB
    heads = q_ref.shape[1] // HD
    scale = math.log2(math.e) / math.sqrt(HD)
    offsets = lax.broadcasted_iota(jnp.int32, (1, KB), 1)
    within = offsets % block_rows * n + offsets // block_rows
    q_within = start % KB + lax.broadcasted_iota(jnp.int32, (tok_rows, 1), 0)

    def item(block, head, masked):
        rows = pl.ds(pl.multiple_of(block * block_rows, block_rows), block_rows)
        k = kv_ref[0, :, rows, :HD].reshape(KB, HD)
        v = kv_ref[0, :, rows, HD:].reshape(KB, HD)
        q = q_ref[:, head * HD : (head + 1) * HD]
        s = lax.dot_general(q, k, (((1,), (1,)), ((), ())), preferred_element_type=jnp.float32)
        if masked:
            s = jnp.where(within <= q_within, s, masked_score)
        peak = jnp.max(s, axis=1, keepdims=True)
        raised = jnp.exp2((s - peak) * scale)
        total = jnp.sum(raised, axis=1, keepdims=True)
        blended = jnp.dot(raised.astype(jnp.bfloat16), v, preferred_element_type=jnp.float32)
        return peak, total, blended

    def more(c, carry):
        merged = []
        for head, (top, total, blended) in enumerate(carry):
            peak_c, total_c, blended_c = item(sel_ref[q_block, c], head, False)
            new = jnp.maximum(top, peak_c)
            old_f = jnp.exp2((top - new) * scale)
            new_f = jnp.exp2((peak_c - new) * scale)
            merged.append((new, total * old_f + total_c * new_f, blended * old_f + blended_c * new_f))
        return tuple(merged)

    carry = tuple(item(q_block, head, True) for head in range(heads))
    carry = lax.fori_loop(1, cnt_ref[q_block], more, carry)
    for head, (_, total, blended) in enumerate(carry):
        out_ref[:, head * HD : (head + 1) * HD] = (blended / total).astype(out_ref.dtype)


def ladder_shards(hidden, queries, weight_buckets, bucket_rows, selected, counts):
    n = lax.axis_size("ctx")
    tok_rows, half = hidden.shape
    buckets = bucket_rows.shape[0]
    depth = half * lax.axis_size("tp") // buckets
    owned, _, kv_local = weight_buckets.shape[:3]
    width = 2 * HD
    w = weight_buckets.reshape(owned, depth, kv_local * width)
    vmem = pl.BlockSpec(memory_space=pltpu.VMEM)
    smem = pl.BlockSpec(memory_space=pltpu.SMEM)
    dma = pltpu.SemaphoreType.DMA
    pieces = tok_rows * n // KB
    f32 = jnp.float32
    bf16 = jnp.bfloat16
    kv = pl.pallas_call(
        functools.partial(project_kernel, n),
        out_shape=jax.ShapeDtypeStruct((kv_local, n, tok_rows, width), bf16),
        in_specs=[smem, vmem, vmem],
        out_specs=vmem,
        scratch_shapes=[
            pltpu.VMEM((buckets, tok_rows, depth), bf16),
            pltpu.VMEM((n, tok_rows, depth), bf16),
            pltpu.VMEM((n // 2, tok_rows, depth), bf16),
            pltpu.VMEM((kv_local, n, depth, width), bf16),
            pltpu.VMEM((kv_local, tok_rows, width), f32),
            pltpu.VMEM((kv_local, tok_rows, width), f32),
            pltpu.VMEM((kv_local, tok_rows, width), f32),
            dma((3, buckets // 2)),
            dma((kv_local, 4, n - 1)), dma((kv_local, 4, n - 1)),
            dma((n // 2,)), dma((n // 2,)), dma((n // 2,)), dma((n // 2,)),
            dma((kv_local,)), dma((kv_local,)),
            dma((kv_local, pieces, n - 1)), dma((kv_local, pieces, n - 1)),
            dma((kv_local,)),
        ],
        compiler_params=pltpu.CompilerParams(
            collective_id=0, has_side_effects=True, vmem_limit_bytes=40 * MIB
        ),
        name="project",
    )(bucket_rows, hidden, w)

    group = queries.shape[1] // kv_local
    here = lax.axis_index("ctx").astype(jnp.int32).reshape(1)
    return pl.pallas_call(
        functools.partial(attend_kernel, n),
        out_shape=jax.ShapeDtypeStruct(queries.shape, bf16),
        grid_spec=pltpu.PrefetchScalarGridSpec(
            num_scalar_prefetch=3,
            grid=(kv_local,),
            in_specs=[
                pl.BlockSpec((tok_rows, group), lambda h, *_: (0, h)),
                pl.BlockSpec((1, n, tok_rows, width), lambda h, *_: (h, 0, 0, 0)),
            ],
            out_specs=pl.BlockSpec((tok_rows, group), lambda h, *_: (0, h)),
        ),
        compiler_params=pltpu.CompilerParams(vmem_limit_bytes=40 * MIB),
        name="attend",
    )(selected, counts, here, queries, kv)


def takes_ladder(mesh, hidden, weight_buckets):
    shape = mesh.shape
    n = shape["ctx"]
    if shape["groups"] != 2 or shape["tp"] != 2 or n % 2 or n > 16:
        return False
    tok_rows = hidden.shape[0] // (2 * n)
    buckets, depth, heads = weight_buckets.shape[:3]
    fits = buckets == 2 * n and depth % (4 * SUB) == 0 and heads == 4
    return fits and KB % tok_rows == 0 and KB // n % SUB == 0


def solution(mesh):
    placed = (
        P(("groups", "ctx"), "tp"),
        P(("groups", "ctx"), "tp"),
        P("ctx", None, "tp", None, None),
        P(),
        P("groups", None),
        P("groups"),
    )

    def run(hidden, queries, weight_buckets, bucket_rows, selected, counts):
        body = ladder_shards if takes_ladder(mesh, hidden, weight_buckets) else general_shards
        return jax.shard_map(
            body, mesh=mesh, in_specs=placed, out_specs=P(("groups", "ctx"), "tp"), check_vma=False
        )(hidden, queries, weight_buckets, bucket_rows, selected, counts)

    return run
```

```python
import functools
import math

import jax
import jax.numpy as jnp
from jax import lax
from jax.experimental import pallas as pl
from jax.experimental.pallas import tpu as pltpu
from jax.sharding import PartitionSpec as P

HD = 128
KB = 512
TOPK = 3


masked_score = -1e30


def general_shards(hidden, queries, weight_buckets, bucket_rows, selected, counts):
    tok_rows = hidden.shape[0]
    ctx_size = lax.axis_size("ctx")
    ctx_index = lax.axis_index("ctx")
    gathered = lax.all_gather(hidden, "tp", axis=1, tiled=True)
    feat_width = gathered.shape[1]
    bucket_count = bucket_rows.shape[0]
    bucket_depth = feat_width // bucket_count
    kv_local = weight_buckets.shape[2]
    kv_width = kv_local * 2 * HD
    arranged = gathered.reshape(tok_rows, bucket_count, bucket_depth)[:, bucket_rows, :]
    arranged = arranged.reshape(tok_rows, feat_width)
    piece = lax.all_gather(weight_buckets, "ctx", axis=0, tiled=True)
    count_rows = piece.shape[0] * bucket_depth
    projected = jnp.dot(
        arranged, piece.reshape(count_rows, kv_width), preferred_element_type=jnp.float32
    )
    key_values = projected.astype(jnp.bfloat16)
    block_count = selected.shape[0]
    block_rows = tok_rows // block_count
    by_block = key_values.reshape(block_count, block_rows, kv_width)
    query_blocks = max(1, tok_rows // KB)
    query_len = min(KB, tok_rows)
    targets = (jnp.arange(ctx_size, dtype=jnp.int32) * tok_rows // KB)[:, None] + jnp.arange(
        query_blocks, dtype=jnp.int32
    )[None, :]
    wanted = selected[targets].reshape(ctx_size, query_blocks * TOPK)
    live = jnp.arange(TOPK, dtype=jnp.int32)[None, None, :] < counts[targets][:, :, None]
    block_tags = jnp.where(live.reshape(ctx_size, query_blocks * TOPK), wanted, -1)
    local_tags = jnp.broadcast_to(
        jnp.arange(query_blocks, dtype=jnp.int32)[:, None], (query_blocks, TOPK)
    )
    local_tags = jnp.broadcast_to(local_tags, block_tags.shape)
    markers = jnp.stack([block_tags, local_tags], axis=-1).astype(jnp.bfloat16)
    outgoing = by_block[wanted]
    heads_local = queries.shape[1] // HD
    group_size = heads_local // kv_local
    score_scale = 1.0 / math.sqrt(HD)
    offsets = jnp.arange(KB, dtype=jnp.int32)
    within = offsets % block_rows * ctx_size + offsets // block_rows
    query_offsets = jnp.arange(query_len, dtype=jnp.int32)

    def one_item(payload, marker):
        block_id = marker[0].astype(jnp.int32)
        is_live = block_id >= 0
        key_block = jnp.maximum(block_id, 0)
        which_block = marker[1].astype(jnp.int32)
        stacked = payload.reshape(KB, kv_local, 2, HD)
        key_pos = key_block * KB + within
        rows_here = queries
        rows_here = rows_here.reshape(query_len, kv_local, group_size, HD)
        query_pos = ctx_index * tok_rows + which_block * query_len + query_offsets
        scores = (
            jnp.einsum(
                "qkgd,skd->kgqs", rows_here, stacked[:, :, 0], preferred_element_type=jnp.float32
            )
            * score_scale
        )
        visible = (key_pos[None, :] <= query_pos[:, None]) & is_live
        scores = jnp.where(visible, scores, masked_score)
        peak = scores.max(axis=-1)
        raised = jnp.exp(scores - peak[..., None])
        total = raised.sum(axis=-1)
        blended = jnp.einsum(
            "kgqs,skd->kgqd",
            raised.astype(jnp.bfloat16),
            stacked[:, :, 1],
            preferred_element_type=jnp.float32,
        )
        return (peak, total, blended)

    payloads = lax.all_to_all(outgoing, "ctx", split_axis=0, concat_axis=0, tiled=True)
    markings = lax.all_to_all(markers, "ctx", split_axis=0, concat_axis=0, tiled=True)

    def handle(position):
        payload = lax.dynamic_index_in_dim(payloads, position, 1, keepdims=False)
        marker = lax.dynamic_index_in_dim(markings[0], position, 0, keepdims=False)
        return one_item(payload, marker)

    peaks, totals, blends = lax.map(handle, jnp.arange(payloads.shape[1], dtype=jnp.int32))
    peaks = peaks.reshape(query_blocks, TOPK, kv_local, group_size, query_len)
    totals = totals.reshape(query_blocks, TOPK, kv_local, group_size, query_len)
    blends = blends.reshape(query_blocks, TOPK, kv_local, group_size, query_len, HD)
    highest = peaks.max(axis=1, keepdims=True)
    factors = jnp.exp(peaks - highest)
    weighted = jnp.sum(factors[..., None] * blends, axis=1)
    normalizer = jnp.sum(factors * totals, axis=1)
    result = weighted / normalizer[..., None]
    return result.transpose(0, 3, 1, 2, 4).reshape(tok_rows, heads_local * HD).astype(jnp.bfloat16)


SUB = 16
MESH = pl.DeviceIdType.MESH
MIB = 1 << 20


def ladder_ctx(pos, n):
    upper = pos // (n // 2)
    return 2 * pos + upper * (2 * n - 1 - 4 * pos)


def ladder_pos(ctx, n):
    return ctx // 2 + (ctx % 2) * (n - 1 - 2 * (ctx // 2))


def project_kernel(
    n, rows_ref, hidden_ref, w_ref, kv_ref,
    feats, xfeats, stage, wbuf, acc, psend, precv,
    hid_sem, w_send, w_recv, x_send, x_recv, f_send, f_recv, p_send, p_recv, kv_send, kv_recv, own_sem,
):
    ctx = lax.axis_index("ctx")
    plane = lax.axis_index("groups")
    core = lax.axis_index("tp")
    col = ctx % 2
    pos = plane * (n - 1) + (ctx // 2) * (1 - 2 * plane)
    walk = ladder_pos(ctx, n)
    after = ladder_ctx((walk + 1) % n, n)
    before = ladder_ctx((walk + n - 1) % n, n)
    depth = feats.shape[2]
    width = wbuf.shape[3]
    in_half = feats.shape[0] // 2
    share = n // 2

    def node(p):
        side = p // (n // 2)
        return side, p * (1 - 2 * side) + side * (n - 1)

    def bucket(p, column):
        side, level = node(p)
        return (level * 2 + column) * 2 + side

    def ring_peer(p):
        side, level = node(p)
        return {"ctx": level * 2 + col, "groups": side}

    up, down = ring_peer((pos + 1) % n), ring_peer((pos + n - 1) % n)
    other_core = {"tp": 1 - core}
    other_col = {"ctx": ctx + 1 - 2 * col}

    barrier = pltpu.get_barrier_semaphore()
    peers = (up, down, other_core, other_col, {"ctx": after}, {"ctx": before})
    for peer in peers:
        pl.semaphore_signal(barrier, inc=1, device_id=peer, device_id_type=MESH)
    pl.semaphore_wait(barrier, len(peers))

    piece = depth // 4

    def weight_copy(c, k, step):
        rows = pl.ds(k * piece, piece)
        if k < 2:
            origin, peer = (pos + n - step) % n, up
        else:
            origin, peer = (pos + step) % n, down
        if step == 0:
            source = w_ref.at[plane, rows, pl.ds(c * width, width)]
        else:
            source = wbuf.at[c, origin, rows]
        return pltpu.make_async_remote_copy(
            src_ref=source, dst_ref=wbuf.at[c, origin, rows],
            send_sem=w_send.at[c, k, step], recv_sem=w_recv.at[c, k, step],
            device_id=peer, device_id_type=MESH,
        )

    def weight_goes(k, step):
        return (2 * pos + (2 + n - step if k < 2 else step)) % n != 0

    def weight_comes(k, step):
        return (2 * pos + (n - step if k < 2 else 2 + step)) % n != 0

    def weight_send(c, k, step):
        @pl.when(weight_goes(k, step))
        def _():
            weight_copy(c, k, step).start()

    def weight_start(c):
        for k in range(4):
            weight_send(c, k, 0)

    def weight_step(c, step):
        for k in range(4):
            @pl.when(weight_comes(k, step))
            def _():
                weight_copy(c, k, step).wait_recv()

            if step + 1 < n - 1:
                weight_send(c, k, step + 1)

    def own_copies(c):
        columns = pl.ds(c * width, width)
        return [
            pltpu.make_async_copy(
                w_ref.at[side, :, columns], wbuf.at[c, spot], own_sem.at[c, i]
            )
            for i, (side, spot) in enumerate(((plane, pos), (1 - plane, n - 1 - pos)))
        ]

    def hidden_copies(i):
        source = hidden_ref.at[:, pl.ds(i * depth, depth)]
        mine = feats.at[core * in_half + i]
        swap = pltpu.make_async_remote_copy(
            src_ref=source, dst_ref=mine, send_sem=hid_sem.at[0, i], recv_sem=hid_sem.at[1, i],
            device_id=other_core, device_id_type=MESH,
        )
        return swap, pltpu.make_async_copy(source, mine, hid_sem.at[2, i])

    def across_copy(i):
        return pltpu.make_async_remote_copy(
            src_ref=stage.at[i], dst_ref=xfeats.at[core * share + i],
            send_sem=x_send.at[i], recv_sem=x_recv.at[i],
            device_id=other_col, device_id_type=MESH,
        )

    def pass_copy(i):
        spot = xfeats.at[core * share + i]
        return pltpu.make_async_remote_copy(
            src_ref=spot, dst_ref=spot, send_sem=f_send.at[i], recv_sem=f_recv.at[i],
            device_id=other_core, device_id_type=MESH,
        )

    def partial_copy(c):
        return pltpu.make_async_remote_copy(
            src_ref=psend.at[c], dst_ref=precv.at[c], send_sem=p_send.at[c], recv_sem=p_recv.at[c],
            device_id=other_col, device_id_type=MESH,
        )

    block_rows = KB // n

    def kv_copy(c, k, step):
        rows = pl.ds(k * block_rows, block_rows)
        if k % 2 == 0:
            origin, peer = ladder_ctx((walk + n - step) % n, n), after
        else:
            origin, peer = ladder_ctx((walk + step) % n, n), before
        spot = kv_ref.at[c, origin, rows]
        return pltpu.make_async_remote_copy(
            src_ref=spot, dst_ref=spot, send_sem=kv_send.at[c, k, step], recv_sem=kv_recv.at[c, k, step],
            device_id={"ctx": peer}, device_id_type=MESH,
        )

    pieces = kv_ref.shape[2] // block_rows

    def partials(c):
        psend[c] = jnp.zeros(psend.shape[1:], jnp.float32)

        @pl.loop(0, n)
        def _(p):
            psend[c] += jnp.dot(xfeats[p], wbuf[c, p], preferred_element_type=jnp.float32)

        partial_copy(c).start()
        acc[c] = jnp.zeros(acc.shape[1:], jnp.float32)

        @pl.loop(0, n)
        def _(p):
            row = rows_ref[bucket(p, col)]
            acc[c] += jnp.dot(feats[row], wbuf[c, p], preferred_element_type=jnp.float32)

    def kv_start(c):
        partial_copy(c).wait_recv()
        kv_ref[c, ctx] = (acc[c] + precv[c]).astype(kv_ref.dtype)
        for k in range(pieces):
            kv_copy(c, k, 0).start()

    def kv_step(c, step):
        for k in range(pieces):
            kv_copy(c, k, step).wait_recv()
            if step + 1 < n - 1:
                kv_copy(c, k, step + 1).start()

    for c in range(2):
        for copy in own_copies(c):
            copy.start()
    weight_start(0)
    for i in range(in_half):
        for copy in hidden_copies(i):
            copy.start()
    for c in range(2):
        for copy in own_copies(c):
            copy.wait()
    steps = n - 1
    lag = 1
    for t in range(steps + lag):
        if t < steps:
            weight_step(0, t)
        if t + 1 == lag:
            weight_start(1)
        if t >= lag:
            weight_step(1, t - lag)
        if t == 1:
            for i in range(in_half):
                for copy in hidden_copies(i):
                    copy.wait()
            for i in range(share):
                stage[i] = feats[rows_ref[bucket(core * share + i, 1 - col)]]
                across_copy(i).start()
        if t == steps + lag - 2:
            for i in range(share):
                across_copy(i).wait_recv()
                pass_copy(i).start()
        if t == steps + lag - 1:
            for i in range(share):
                pass_copy(i).wait_recv()
            partials(0)
    partials(1)
    for c in range(2):
        kv_start(c)
    for t in range(steps):
        for c in range(2):
            kv_step(c, t)

    for i in range(share):
        across_copy(i).wait_send()
        pass_copy(i).wait_send()
    for c in range(2):
        partial_copy(c).wait_send()
        for s in range(steps):
            for k in range(4):
                @pl.when(weight_goes(k, s))
                def _():
                    weight_copy(c, k, s).wait_send()

            for k in range(pieces):
                kv_copy(c, k, s).wait_send()


def attend_kernel(n, sel_ref, cnt_ref, at_ref, q_ref, kv_ref, out_ref):
    tok_rows = q_ref.shape[0]
    block_rows = KB // n
    start = at_ref[0] * tok_rows
    q_block = start // KB
    heads = q_ref.shape[1] // HD
    scale = math.log2(math.e) / math.sqrt(HD)
    offsets = lax.broadcasted_iota(jnp.int32, (1, KB), 1)
    within = offsets % block_rows * n + offsets // block_rows
    q_within = start % KB + lax.broadcasted_iota(jnp.int32, (tok_rows, 1), 0)

    def item(block, head, masked):
        rows = pl.ds(pl.multiple_of(block * block_rows, block_rows), block_rows)
        k = kv_ref[0, :, rows, :HD].reshape(KB, HD)
        v = kv_ref[0, :, rows, HD:].reshape(KB, HD)
        q = q_ref[:, head * HD : (head + 1) * HD]
        s = lax.dot_general(q, k, (((1,), (1,)), ((), ())), preferred_element_type=jnp.float32)
        if masked:
            s = jnp.where(within <= q_within, s, masked_score)
        peak = jnp.max(s, axis=1, keepdims=True)
        raised = jnp.exp2((s - peak) * scale)
        total = jnp.sum(raised, axis=1, keepdims=True)
        blended = jnp.dot(raised.astype(jnp.bfloat16), v, preferred_element_type=jnp.float32)
        return peak, total, blended

    def more(c, carry):
        merged = []
        for head, (top, total, blended) in enumerate(carry):
            peak_c, total_c, blended_c = item(sel_ref[q_block, c], head, False)
            new = jnp.maximum(top, peak_c)
            old_f = jnp.exp2((top - new) * scale)
            new_f = jnp.exp2((peak_c - new) * scale)
            merged.append((new, total * old_f + total_c * new_f, blended * old_f + blended_c * new_f))
        return tuple(merged)

    carry = tuple(item(q_block, head, True) for head in range(heads))
    carry = lax.fori_loop(1, cnt_ref[q_block], more, carry)
    for head, (_, total, blended) in enumerate(carry):
        out_ref[:, head * HD : (head + 1) * HD] = (blended / total).astype(out_ref.dtype)


def ladder_shards(hidden, queries, weight_buckets, bucket_rows, selected, counts):
    n = lax.axis_size("ctx")
    tok_rows, half = hidden.shape
    buckets = bucket_rows.shape[0]
    depth = half * lax.axis_size("tp") // buckets
    owned, _, kv_local = weight_buckets.shape[:3]
    width = 2 * HD
    w = weight_buckets.reshape(owned, depth, kv_local * width)
    vmem = pl.BlockSpec(memory_space=pltpu.VMEM)
    smem = pl.BlockSpec(memory_space=pltpu.SMEM)
    dma = pltpu.SemaphoreType.DMA
    pieces = tok_rows * n // KB
    f32 = jnp.float32
    bf16 = jnp.bfloat16
    kv = pl.pallas_call(
        functools.partial(project_kernel, n),
        out_shape=jax.ShapeDtypeStruct((kv_local, n, tok_rows, width), bf16),
        in_specs=[smem, vmem, vmem],
        out_specs=vmem,
        scratch_shapes=[
            pltpu.VMEM((buckets, tok_rows, depth), bf16),
            pltpu.VMEM((n, tok_rows, depth), bf16),
            pltpu.VMEM((n // 2, tok_rows, depth), bf16),
            pltpu.VMEM((kv_local, n, depth, width), bf16),
            pltpu.VMEM((kv_local, tok_rows, width), f32),
            pltpu.VMEM((kv_local, tok_rows, width), f32),
            pltpu.VMEM((kv_local, tok_rows, width), f32),
            dma((3, buckets // 2)),
            dma((kv_local, 4, n - 1)), dma((kv_local, 4, n - 1)),
            dma((n // 2,)), dma((n // 2,)), dma((n // 2,)), dma((n // 2,)),
            dma((kv_local,)), dma((kv_local,)),
            dma((kv_local, pieces, n - 1)), dma((kv_local, pieces, n - 1)),
            dma((kv_local, 2)),
        ],
        compiler_params=pltpu.CompilerParams(
            collective_id=0, has_side_effects=True, vmem_limit_bytes=40 * MIB
        ),
        name="project",
    )(bucket_rows, hidden, w)

    group = queries.shape[1] // kv_local
    here = lax.axis_index("ctx").astype(jnp.int32).reshape(1)
    return pl.pallas_call(
        functools.partial(attend_kernel, n),
        out_shape=jax.ShapeDtypeStruct(queries.shape, bf16),
        grid_spec=pltpu.PrefetchScalarGridSpec(
            num_scalar_prefetch=3,
            grid=(kv_local,),
            in_specs=[
                pl.BlockSpec((tok_rows, group), lambda h, *_: (0, h)),
                pl.BlockSpec((1, n, tok_rows, width), lambda h, *_: (h, 0, 0, 0)),
            ],
            out_specs=pl.BlockSpec((tok_rows, group), lambda h, *_: (0, h)),
        ),
        compiler_params=pltpu.CompilerParams(vmem_limit_bytes=40 * MIB),
        name="attend",
    )(selected, counts, here, queries, kv)


def takes_ladder(mesh, hidden, weight_buckets):
    shape = mesh.shape
    n = shape["ctx"]
    if shape["groups"] != 2 or shape["tp"] != 2 or n % 2 or n > 16:
        return False
    tok_rows = hidden.shape[0] // (2 * n)
    buckets, depth, heads = weight_buckets.shape[:3]
    fits = buckets == 2 * n and depth % (4 * SUB) == 0 and heads == 4
    return fits and KB % tok_rows == 0 and KB // n % SUB == 0


def solution(mesh):
    placed = (
        P(("groups", "ctx"), "tp"),
        P(("groups", "ctx"), "tp"),
        P("ctx", None, "tp", None, None),
        P(),
        P("groups", None),
        P("groups"),
    )

    def run(hidden, queries, weight_buckets, bucket_rows, selected, counts):
        body = ladder_shards if takes_ladder(mesh, hidden, weight_buckets) else general_shards
        return jax.shard_map(
            body, mesh=mesh, in_specs=placed, out_specs=P(("groups", "ctx"), "tp"), check_vma=False
        )(hidden, queries, weight_buckets, bucket_rows, selected, counts)

    return run
```

```python
import functools
import math

import jax
import jax.numpy as jnp
from jax import lax
from jax.experimental import pallas as pl
from jax.experimental.pallas import tpu as pltpu
from jax.sharding import PartitionSpec as P

HD = 128
KB = 512
TOPK = 3


masked_score = -1e30


def general_shards(hidden, queries, weight_buckets, bucket_rows, selected, counts):
    tok_rows = hidden.shape[0]
    ctx_size = lax.axis_size("ctx")
    ctx_index = lax.axis_index("ctx")
    gathered = lax.all_gather(hidden, "tp", axis=1, tiled=True)
    feat_width = gathered.shape[1]
    bucket_count = bucket_rows.shape[0]
    bucket_depth = feat_width // bucket_count
    kv_local = weight_buckets.shape[2]
    kv_width = kv_local * 2 * HD
    arranged = gathered.reshape(tok_rows, bucket_count, bucket_depth)[:, bucket_rows, :]
    arranged = arranged.reshape(tok_rows, feat_width)
    piece = lax.all_gather(weight_buckets, "ctx", axis=0, tiled=True)
    count_rows = piece.shape[0] * bucket_depth
    projected = jnp.dot(
        arranged, piece.reshape(count_rows, kv_width), preferred_element_type=jnp.float32
    )
    key_values = projected.astype(jnp.bfloat16)
    block_count = selected.shape[0]
    block_rows = tok_rows // block_count
    by_block = key_values.reshape(block_count, block_rows, kv_width)
    query_blocks = max(1, tok_rows // KB)
    query_len = min(KB, tok_rows)
    targets = (jnp.arange(ctx_size, dtype=jnp.int32) * tok_rows // KB)[:, None] + jnp.arange(
        query_blocks, dtype=jnp.int32
    )[None, :]
    wanted = selected[targets].reshape(ctx_size, query_blocks * TOPK)
    live = jnp.arange(TOPK, dtype=jnp.int32)[None, None, :] < counts[targets][:, :, None]
    block_tags = jnp.where(live.reshape(ctx_size, query_blocks * TOPK), wanted, -1)
    local_tags = jnp.broadcast_to(
        jnp.arange(query_blocks, dtype=jnp.int32)[:, None], (query_blocks, TOPK)
    )
    local_tags = jnp.broadcast_to(local_tags, block_tags.shape)
    markers = jnp.stack([block_tags, local_tags], axis=-1).astype(jnp.bfloat16)
    outgoing = by_block[wanted]
    heads_local = queries.shape[1] // HD
    group_size = heads_local // kv_local
    score_scale = 1.0 / math.sqrt(HD)
    offsets = jnp.arange(KB, dtype=jnp.int32)
    within = offsets % block_rows * ctx_size + offsets // block_rows
    query_offsets = jnp.arange(query_len, dtype=jnp.int32)

    def one_item(payload, marker):
        block_id = marker[0].astype(jnp.int32)
        is_live = block_id >= 0
        key_block = jnp.maximum(block_id, 0)
        which_block = marker[1].astype(jnp.int32)
        stacked = payload.reshape(KB, kv_local, 2, HD)
        key_pos = key_block * KB + within
        rows_here = queries
        rows_here = rows_here.reshape(query_len, kv_local, group_size, HD)
        query_pos = ctx_index * tok_rows + which_block * query_len + query_offsets
        scores = (
            jnp.einsum(
                "qkgd,skd->kgqs", rows_here, stacked[:, :, 0], preferred_element_type=jnp.float32
            )
            * score_scale
        )
        visible = (key_pos[None, :] <= query_pos[:, None]) & is_live
        scores = jnp.where(visible, scores, masked_score)
        peak = scores.max(axis=-1)
        raised = jnp.exp(scores - peak[..., None])
        total = raised.sum(axis=-1)
        blended = jnp.einsum(
            "kgqs,skd->kgqd",
            raised.astype(jnp.bfloat16),
            stacked[:, :, 1],
            preferred_element_type=jnp.float32,
        )
        return (peak, total, blended)

    payloads = lax.all_to_all(outgoing, "ctx", split_axis=0, concat_axis=0, tiled=True)
    markings = lax.all_to_all(markers, "ctx", split_axis=0, concat_axis=0, tiled=True)

    def handle(position):
        payload = lax.dynamic_index_in_dim(payloads, position, 1, keepdims=False)
        marker = lax.dynamic_index_in_dim(markings[0], position, 0, keepdims=False)
        return one_item(payload, marker)

    peaks, totals, blends = lax.map(handle, jnp.arange(payloads.shape[1], dtype=jnp.int32))
    peaks = peaks.reshape(query_blocks, TOPK, kv_local, group_size, query_len)
    totals = totals.reshape(query_blocks, TOPK, kv_local, group_size, query_len)
    blends = blends.reshape(query_blocks, TOPK, kv_local, group_size, query_len, HD)
    highest = peaks.max(axis=1, keepdims=True)
    factors = jnp.exp(peaks - highest)
    weighted = jnp.sum(factors[..., None] * blends, axis=1)
    normalizer = jnp.sum(factors * totals, axis=1)
    result = weighted / normalizer[..., None]
    return result.transpose(0, 3, 1, 2, 4).reshape(tok_rows, heads_local * HD).astype(jnp.bfloat16)


SUB = 16
MESH = pl.DeviceIdType.MESH
MIB = 1 << 20


def ladder_ctx(pos, n):
    upper = pos // (n // 2)
    return 2 * pos + upper * (2 * n - 1 - 4 * pos)


def ladder_pos(ctx, n):
    return ctx // 2 + (ctx % 2) * (n - 1 - 2 * (ctx // 2))


def project_kernel(
    n, rows_ref, hidden_ref, w_ref, kv_ref,
    feats, xfeats, stage, wbuf, acc, psend, precv,
    hid_sem, w_send, w_recv, x_send, x_recv, f_send, f_recv, p_send, p_recv, kv_send, kv_recv, own_sem,
):
    ctx = lax.axis_index("ctx")
    plane = lax.axis_index("groups")
    core = lax.axis_index("tp")
    col = ctx % 2
    pos = plane * (n - 1) + (ctx // 2) * (1 - 2 * plane)
    walk = ladder_pos(ctx, n)
    after = ladder_ctx((walk + 1) % n, n)
    before = ladder_ctx((walk + n - 1) % n, n)
    depth = feats.shape[2]
    width = wbuf.shape[3]
    in_half = feats.shape[0] // 2
    share = n // 2

    def node(p):
        side = p // (n // 2)
        return side, p * (1 - 2 * side) + side * (n - 1)

    def bucket(p, column):
        side, level = node(p)
        return (level * 2 + column) * 2 + side

    def ring_peer(p):
        side, level = node(p)
        return {"ctx": level * 2 + col, "groups": side}

    up, down = ring_peer((pos + 1) % n), ring_peer((pos + n - 1) % n)
    other_core = {"tp": 1 - core}
    other_col = {"ctx": ctx + 1 - 2 * col}

    barrier = pltpu.get_barrier_semaphore()
    peers = (up, down, other_core, other_col, {"ctx": after}, {"ctx": before})
    for peer in peers:
        pl.semaphore_signal(barrier, inc=1, device_id=peer, device_id_type=MESH)
    pl.semaphore_wait(barrier, len(peers))

    piece = depth // 4

    def weight_copy(c, k, step):
        rows = pl.ds(k * piece, piece)
        if k < 2:
            origin, peer = (pos + n - step) % n, up
        else:
            origin, peer = (pos + step) % n, down
        if step == 0:
            source = w_ref.at[plane, rows, pl.ds(c * width, width)]
        else:
            source = wbuf.at[c, origin, rows]
        return pltpu.make_async_remote_copy(
            src_ref=source, dst_ref=wbuf.at[c, origin, rows],
            send_sem=w_send.at[c, k, step], recv_sem=w_recv.at[c, k, step],
            device_id=peer, device_id_type=MESH,
        )

    def weight_goes(k, step):
        return (2 * pos + (2 + n - step if k < 2 else step)) % n != 0

    def weight_comes(k, step):
        return (2 * pos + (n - step if k < 2 else 2 + step)) % n != 0

    def weight_send(c, k, step):
        @pl.when(weight_goes(k, step))
        def _():
            weight_copy(c, k, step).start()

    def weight_start(c):
        for k in range(4):
            weight_send(c, k, 0)

    def weight_step(c, step):
        for k in range(4):
            @pl.when(weight_comes(k, step))
            def _():
                weight_copy(c, k, step).wait_recv()

            if step + 1 < n - 1:
                weight_send(c, k, step + 1)

    def own_copies(c):
        columns = pl.ds(c * width, width)
        return [
            pltpu.make_async_copy(
                w_ref.at[side, :, columns], wbuf.at[c, spot], own_sem.at[c, i]
            )
            for i, (side, spot) in enumerate(((plane, pos), (1 - plane, n - 1 - pos)))
        ]

    def hidden_copies(i):
        source = hidden_ref.at[:, pl.ds(i * depth, depth)]
        mine = feats.at[core * in_half + i]
        swap = pltpu.make_async_remote_copy(
            src_ref=source, dst_ref=mine, send_sem=hid_sem.at[0, i], recv_sem=hid_sem.at[1, i],
            device_id=other_core, device_id_type=MESH,
        )
        return swap, pltpu.make_async_copy(source, mine, hid_sem.at[2, i])

    def across_copy(i):
        return pltpu.make_async_remote_copy(
            src_ref=stage.at[i], dst_ref=xfeats.at[core * share + i],
            send_sem=x_send.at[i], recv_sem=x_recv.at[i],
            device_id=other_col, device_id_type=MESH,
        )

    def pass_copy(i):
        spot = xfeats.at[core * share + i]
        return pltpu.make_async_remote_copy(
            src_ref=spot, dst_ref=spot, send_sem=f_send.at[i], recv_sem=f_recv.at[i],
            device_id=other_core, device_id_type=MESH,
        )

    def partial_copy(c):
        return pltpu.make_async_remote_copy(
            src_ref=psend.at[c], dst_ref=precv.at[c], send_sem=p_send.at[c], recv_sem=p_recv.at[c],
            device_id=other_col, device_id_type=MESH,
        )

    block_rows = KB // n

    def kv_copy(c, k, step):
        rows = pl.ds(k * block_rows, block_rows)
        if k % 2 == 0:
            origin, peer = ladder_ctx((walk + n - step) % n, n), after
        else:
            origin, peer = ladder_ctx((walk + step) % n, n), before
        spot = kv_ref.at[c, origin, rows]
        return pltpu.make_async_remote_copy(
            src_ref=spot, dst_ref=spot, send_sem=kv_send.at[c, k, step], recv_sem=kv_recv.at[c, k, step],
            device_id={"ctx": peer}, device_id_type=MESH,
        )

    pieces = kv_ref.shape[2] // block_rows

    def partials(c):
        psend[c] = jnp.zeros(psend.shape[1:], jnp.float32)

        @pl.loop(0, n)
        def _(p):
            psend[c] += jnp.dot(xfeats[p], wbuf[c, p], preferred_element_type=jnp.float32)

        partial_copy(c).start()

    def own_sums(c):
        acc[c] = jnp.zeros(acc.shape[1:], jnp.float32)

        @pl.loop(0, n)
        def _(p):
            row = rows_ref[bucket(p, col)]
            acc[c] += jnp.dot(feats[row], wbuf[c, p], preferred_element_type=jnp.float32)

    def kv_start(c):
        partial_copy(c).wait_recv()
        kv_ref[c, ctx] = (acc[c] + precv[c]).astype(kv_ref.dtype)
        for k in range(pieces):
            kv_copy(c, k, 0).start()

    def kv_step(c, step):
        for k in range(pieces):
            kv_copy(c, k, step).wait_recv()
            if step + 1 < n - 1:
                kv_copy(c, k, step + 1).start()

    for c in range(2):
        for copy in own_copies(c):
            copy.start()
    weight_start(0)
    for i in range(in_half):
        for copy in hidden_copies(i):
            copy.start()
    for c in range(2):
        for copy in own_copies(c):
            copy.wait()
    steps = n - 1
    lag = 1
    for t in range(steps + lag):
        if t < steps:
            weight_step(0, t)
        if t + 1 == lag:
            weight_start(1)
        if t >= lag:
            weight_step(1, t - lag)
        if t == 1:
            for i in range(in_half):
                for copy in hidden_copies(i):
                    copy.wait()
            for i in range(share):
                stage[i] = feats[rows_ref[bucket(core * share + i, 1 - col)]]
                across_copy(i).start()
        if t == steps + lag - 2:
            for i in range(share):
                across_copy(i).wait_recv()
                pass_copy(i).start()
        if t == steps + lag - 1:
            for i in range(share):
                pass_copy(i).wait_recv()
            partials(0)
    partials(1)
    for c in range(2):
        own_sums(c)
    for c in range(2):
        kv_start(c)
    for t in range(steps):
        for c in range(2):
            kv_step(c, t)

    for i in range(share):
        across_copy(i).wait_send()
        pass_copy(i).wait_send()
    for c in range(2):
        partial_copy(c).wait_send()
        for s in range(steps):
            for k in range(4):
                @pl.when(weight_goes(k, s))
                def _():
                    weight_copy(c, k, s).wait_send()

            for k in range(pieces):
                kv_copy(c, k, s).wait_send()


def attend_kernel(n, sel_ref, cnt_ref, at_ref, q_ref, kv_ref, out_ref):
    tok_rows = q_ref.shape[0]
    block_rows = KB // n
    start = at_ref[0] * tok_rows
    q_block = start // KB
    heads = q_ref.shape[1] // HD
    scale = math.log2(math.e) / math.sqrt(HD)
    offsets = lax.broadcasted_iota(jnp.int32, (1, KB), 1)
    within = offsets % block_rows * n + offsets // block_rows
    q_within = start % KB + lax.broadcasted_iota(jnp.int32, (tok_rows, 1), 0)

    def item(block, head, masked):
        rows = pl.ds(pl.multiple_of(block * block_rows, block_rows), block_rows)
        k = kv_ref[0, :, rows, :HD].reshape(KB, HD)
        v = kv_ref[0, :, rows, HD:].reshape(KB, HD)
        q = q_ref[:, head * HD : (head + 1) * HD]
        s = lax.dot_general(q, k, (((1,), (1,)), ((), ())), preferred_element_type=jnp.float32)
        if masked:
            s = jnp.where(within <= q_within, s, masked_score)
        peak = jnp.max(s, axis=1, keepdims=True)
        raised = jnp.exp2((s - peak) * scale)
        total = jnp.sum(raised, axis=1, keepdims=True)
        blended = jnp.dot(raised.astype(jnp.bfloat16), v, preferred_element_type=jnp.float32)
        return peak, total, blended

    def more(c, carry):
        merged = []
        for head, (top, total, blended) in enumerate(carry):
            peak_c, total_c, blended_c = item(sel_ref[q_block, c], head, False)
            new = jnp.maximum(top, peak_c)
            old_f = jnp.exp2((top - new) * scale)
            new_f = jnp.exp2((peak_c - new) * scale)
            merged.append((new, total * old_f + total_c * new_f, blended * old_f + blended_c * new_f))
        return tuple(merged)

    carry = tuple(item(q_block, head, True) for head in range(heads))
    carry = lax.fori_loop(1, cnt_ref[q_block], more, carry)
    for head, (_, total, blended) in enumerate(carry):
        out_ref[:, head * HD : (head + 1) * HD] = (blended / total).astype(out_ref.dtype)


def ladder_shards(hidden, queries, weight_buckets, bucket_rows, selected, counts):
    n = lax.axis_size("ctx")
    tok_rows, half = hidden.shape
    buckets = bucket_rows.shape[0]
    depth = half * lax.axis_size("tp") // buckets
    owned, _, kv_local = weight_buckets.shape[:3]
    width = 2 * HD
    w = weight_buckets.reshape(owned, depth, kv_local * width)
    vmem = pl.BlockSpec(memory_space=pltpu.VMEM)
    smem = pl.BlockSpec(memory_space=pltpu.SMEM)
    dma = pltpu.SemaphoreType.DMA
    pieces = tok_rows * n // KB
    f32 = jnp.float32
    bf16 = jnp.bfloat16
    kv = pl.pallas_call(
        functools.partial(project_kernel, n),
        out_shape=jax.ShapeDtypeStruct((kv_local, n, tok_rows, width), bf16),
        in_specs=[smem, vmem, vmem],
        out_specs=vmem,
        scratch_shapes=[
            pltpu.VMEM((buckets, tok_rows, depth), bf16),
            pltpu.VMEM((n, tok_rows, depth), bf16),
            pltpu.VMEM((n // 2, tok_rows, depth), bf16),
            pltpu.VMEM((kv_local, n, depth, width), bf16),
            pltpu.VMEM((kv_local, tok_rows, width), f32),
            pltpu.VMEM((kv_local, tok_rows, width), f32),
            pltpu.VMEM((kv_local, tok_rows, width), f32),
            dma((3, buckets // 2)),
            dma((kv_local, 4, n - 1)), dma((kv_local, 4, n - 1)),
            dma((n // 2,)), dma((n // 2,)), dma((n // 2,)), dma((n // 2,)),
            dma((kv_local,)), dma((kv_local,)),
            dma((kv_local, pieces, n - 1)), dma((kv_local, pieces, n - 1)),
            dma((kv_local, 2)),
        ],
        compiler_params=pltpu.CompilerParams(
            collective_id=0, has_side_effects=True, vmem_limit_bytes=40 * MIB
        ),
        name="project",
    )(bucket_rows, hidden, w)

    group = queries.shape[1] // kv_local
    here = lax.axis_index("ctx").astype(jnp.int32).reshape(1)
    return pl.pallas_call(
        functools.partial(attend_kernel, n),
        out_shape=jax.ShapeDtypeStruct(queries.shape, bf16),
        grid_spec=pltpu.PrefetchScalarGridSpec(
            num_scalar_prefetch=3,
            grid=(kv_local,),
            in_specs=[
                pl.BlockSpec((tok_rows, group), lambda h, *_: (0, h)),
                pl.BlockSpec((1, n, tok_rows, width), lambda h, *_: (h, 0, 0, 0)),
            ],
            out_specs=pl.BlockSpec((tok_rows, group), lambda h, *_: (0, h)),
        ),
        compiler_params=pltpu.CompilerParams(vmem_limit_bytes=40 * MIB),
        name="attend",
    )(selected, counts, here, queries, kv)


def takes_ladder(mesh, hidden, weight_buckets):
    shape = mesh.shape
    n = shape["ctx"]
    if shape["groups"] != 2 or shape["tp"] != 2 or n % 2 or n > 16:
        return False
    tok_rows = hidden.shape[0] // (2 * n)
    buckets, depth, heads = weight_buckets.shape[:3]
    fits = buckets == 2 * n and depth % (4 * SUB) == 0 and heads == 4
    return fits and KB % tok_rows == 0 and KB // n % SUB == 0


def solution(mesh):
    placed = (
        P(("groups", "ctx"), "tp"),
        P(("groups", "ctx"), "tp"),
        P("ctx", None, "tp", None, None),
        P(),
        P("groups", None),
        P("groups"),
    )

    def run(hidden, queries, weight_buckets, bucket_rows, selected, counts):
        body = ladder_shards if takes_ladder(mesh, hidden, weight_buckets) else general_shards
        return jax.shard_map(
            body, mesh=mesh, in_specs=placed, out_specs=P(("groups", "ctx"), "tp"), check_vma=False
        )(hidden, queries, weight_buckets, bucket_rows, selected, counts)

    return run
```
